32 devices in a mesh: batch: 2 (over x), feat: 16 (over z, y, core).
Axes of the slice: x: 2, y: 2, z: 4, core: 2. Of those that a mesh axis runs over, the one named last changes fastest.
Arguments:
- features: bfloat16 [2, 1024, 16384], P('batch', 'feat'), may hold values from -6 to 6
- tile_values: bfloat16 [2, 256, 128, 128], P('batch'), may hold values from 0 to 1.5, as said below
- tile_blocks: int32 [2, 2, 256], P('batch'), may hold values from 0 to 127, as said below
- tile_count: int32 [2], P('batch'), may hold values from 32 to 256, as said below
- w_self: bfloat16 [1024, 512], replicated, may hold values from -0.1875 to 0.1875
- w_neigh: bfloat16 [1024, 512], replicated, may hold values from -0.1875 to 0.1875
- grad_out: bfloat16 [2, 16384, 512], P('batch', 'feat'), may hold values from -0.03125 to 0.03125
Outputs:
- hidden_out: bfloat16 [2, 16384, 512], P('batch', 'feat')
- grad_w: float32 [1024, 2, 512], P('feat')
The draws below stay inside these ranges and needn't reach their ends.
Inputs may be any that keep to these rules, and one draw needn't show every extreme that they name: `tile_values`: at most 30 in 100 entries are nonzero on average; nonzero entries are positive. `tile_blocks`: block indices of tiles; slots at or past the tile count hold arbitrary blocks. `tile_count`: some minibatch uses all 256 slots in every draw.
All inputs are finite; a program needn't handle non-finite values.
Results may differ from the reference program's by a relative error of at most 0.0022.
Values may be sent and summed in bfloat16 or wider, within the bound.
A program may use at most 128 MiB of HBM per device.

```python
import math
import jax
import jax.numpy as jnp
from jax import lax

F = 1024
H = 512
BLOCK = 128
NODES = 16384
NB = 128
TMAX = 256
N_BATCH = 2


def draw_tile_values(key, part):
    key = jax.random.fold_in(key, 11)
    first, second = jax.random.split(key)
    shape = (N_BATCH, TMAX, BLOCK, BLOCK)
    keep = jax.random.uniform(first, shape, dtype=jnp.float32) < 0.3
    values = jnp.exp(jax.random.uniform(second, shape, dtype=jnp.float32, minval=math.log(0.2), maxval=0.0))
    return jnp.where(keep, values, 0.0).astype(jnp.bfloat16)


def draw_tile_blocks(key, part):
    key = jax.random.fold_in(key, 12)
    blocks = jax.random.randint(key, (N_BATCH, 2, TMAX), 0, NB, dtype=jnp.int32)
    blocks = blocks.at[:, 0, 0].set(NB - 1)
    blocks = blocks.at[:, 1, 0].set(0)
    return blocks


def draw_tile_count(key, part):
    key = jax.random.fold_in(key, 13)
    first, second = jax.random.split(key)
    lowest = TMAX // 8
    spread = TMAX - lowest
    order = jax.random.permutation(first, spread).astype(jnp.int32)
    picks = jnp.arange(N_BATCH, dtype=jnp.int32) % spread
    counts = lowest + order[picks]
    busiest = jax.random.randint(second, (), 0, N_BATCH, dtype=jnp.int32)
    return jnp.where(jnp.arange(N_BATCH, dtype=jnp.int32) == busiest, TMAX, counts).astype(jnp.int32)


def steps_of(rng, extent, shards, smallest, largest):
    factor_of = 1.0
    for dim, blocks in shards:
        steps = jax.random.uniform(jax.random.fold_in(jax.random.fold_in(rng, 6), dim), (blocks,), jnp.float32, smallest / len(shards), largest / len(shards))
        factor_of = factor_of * jnp.repeat(jnp.exp(steps), extent[dim] // blocks).reshape((-1,) + (1,) * (len(extent) - 1 - dim))
    return factor_of


def gaussian(stream_key, extent, scale, reach, pieces=(), held_as=jnp.bfloat16):
    result = jax.random.normal(stream_key, extent, jnp.float32) * scale
    if len(pieces) > 0:
        result = steps_of(stream_key, extent, pieces, -0.22, 0.18) * result
    return jnp.clip(result, min=-reach, max=reach).astype(held_as)


def setup_inputs(seed: int = 0) -> dict:
    keys = jax.random.split(jax.random.key(seed), 8)
    return {
        "features": gaussian(keys[0], (N_BATCH, F, NODES), 1.0, 6.0, ((0, 2), (1, 16))),
        "tile_values": draw_tile_values(jax.random.fold_in(keys[7], 71), 0),
        "tile_blocks": draw_tile_blocks(jax.random.fold_in(keys[7], 71), 0),
        "tile_count": draw_tile_count(jax.random.fold_in(keys[7], 71), 0),
        "w_self": gaussian(keys[4], (F, H), F ** -0.5, 0.1875),
        "w_neigh": gaussian(keys[5], (F, H), F ** -0.5, 0.1875),
        "grad_out": gaussian(keys[6], (N_BATCH, NODES, H), (NODES * N_BATCH) ** -0.5, 0.03125, ((0, 2), (1, 16))),
    }


def one_batch(args):
    feats, tiles, blocks, count, w_self, w_neigh, grad = args
    slots = jnp.arange(TMAX, dtype=jnp.int32)
    valid = (slots < count).astype(jnp.float32)
    used = tiles.astype(jnp.float32) * valid[:, None, None]
    dst = blocks[0].astype(jnp.int32)
    src = blocks[1].astype(jnp.int32)
    featf = feats.astype(jnp.float32)
    sources = featf.reshape(F, NB, BLOCK)[:, src, :]
    contrib = jnp.einsum('ftb,tdb->tfd', sources, used)
    summed = jax.ops.segment_sum(contrib, dst, num_segments=NB)
    summed = summed.transpose(1, 0, 2).reshape(F, NODES)
    degree = jax.ops.segment_sum(jnp.sum(used, axis=-1), dst, num_segments=NB).reshape(NODES)
    neigh_mean = (summed / jnp.maximum(degree, 1.0)[None, :]).astype(jnp.bfloat16)
    pre = jnp.dot(feats.T, w_self, preferred_element_type=jnp.float32)
    pre = pre + jnp.dot(neigh_mean.T, w_neigh, preferred_element_type=jnp.float32)
    lowered = jnp.minimum(pre, 0.0)
    hidden = jnp.where(pre > 0, pre, jnp.expm1(lowered)).astype(jnp.bfloat16)
    slope = jnp.where(pre > 0, 1.0, jnp.exp(lowered))
    slope_grad = (grad.astype(jnp.float32) * slope).astype(jnp.bfloat16)
    grad_self = jnp.dot(feats, slope_grad, preferred_element_type=jnp.float32)
    grad_neigh = jnp.dot(neigh_mean, slope_grad, preferred_element_type=jnp.float32)
    return hidden, jnp.stack([grad_self, grad_neigh], axis=1)


def reference(features, tile_values, tile_blocks, tile_count, w_self, w_neigh, grad_out):
    def runner(items):
        feats, tiles, blocks, count, grad = items
        return one_batch((feats, tiles, blocks, count, w_self, w_neigh, grad))
    hidden, grads = lax.map(runner, (features, tile_values, tile_blocks, tile_count, grad_out))
    return hidden, jnp.sum(grads, axis=0)
```

```python
import functools

import jax
import jax.numpy as jnp
from jax import lax
from jax.experimental import pallas as pl
from jax.experimental.pallas import tpu as pltpu
from jax.sharding import PartitionSpec as P

F32 = jnp.float32
BF16 = jnp.bfloat16
NC = 2
UNROLL = 8
NBLK = 256


def kernel(
    dims,
    tile_ref, src_ref, keep_ref, last_ref, has_ref, feat_hbm, tiles_hbm, ws_hbm, wn_hbm, go_hbm,
    hid_ref, gw_ref,
    feat_v, tiles_v, w_v, go_v, pref, msend, xs, pre_v, sg_v, grad,
    s1_send, s1_recv, s2_send, s2_recv, s3_send, s3_recv, s4_send, s4_recv, s5_send, s5_recv,
    load_sem, own_sem, x_send, x_recv, s1_sems, s2_sems, s3_sems, s4_sems, s5_sems,
):
    feat, batch, hi_n, mid_n, rows, nodes, width, slots, hid = dims
    chunk = nodes // NC
    per_chunk = chunk // width
    blocks_per_dev = nodes // width
    me = lax.axis_index("feat")
    mb = lax.axis_index("batch")
    hi = me // (2 * mid_n)
    mid = (me // 2) % mid_n
    core = me % 2

    def slot_of(p):
        return (p % 2) * (feat // 2) + ((p // 2) % mid_n) * hi_n + p // (2 * mid_n)

    my_rows = pl.ds(pl.multiple_of(slot_of(me) * rows, rows), rows)

    def peer(k):
        return (me + 1 + (k + feat // 2 - 1) % (feat - 1)) % feat

    loads = [
        pltpu.make_async_copy(tiles_hbm, tiles_v, load_sem.at[1]),
        pltpu.make_async_copy(go_hbm, go_v, load_sem.at[2]),
    ]
    for cp in loads:
        cp.start()

    barrier = pltpu.get_barrier_semaphore()

    def greet(k, carry):
        pl.semaphore_signal(barrier, inc=1, device_id={"feat": peer(k)}, device_id_type=pl.DeviceIdType.MESH)
        return carry

    lax.fori_loop(0, feat - 1, greet, 0)
    for j in range(1, batch):
        pl.semaphore_signal(
            barrier, inc=1, device_id={"batch": (mb + j) % batch}, device_id_type=pl.DeviceIdType.MESH
        )
    pl.semaphore_wait(barrier, feat - 1 + batch - 1)

    def x_copy(kind, c, k):
        p = peer(k)
        if kind == 0:
            start = pl.multiple_of(p * nodes + c * chunk, chunk)
            src = feat_hbm.at[:, pl.ds(start, chunk)]
        else:
            src = msend.at[c, p]
        return pltpu.make_async_remote_copy(
            src_ref=src,
            dst_ref=xs.at[kind, c, my_rows, :],
            send_sem=x_send.at[kind, c, k],
            recv_sem=x_recv.at[kind, c, me],
            device_id={"feat": p},
            device_id_type=pl.DeviceIdType.MESH,
        )

    for c in range(NC):
        def send_feat(k, carry, c=c):
            x_copy(0, c, k).start()
            return carry
        lax.fori_loop(0, feat - 1, send_feat, 0)

    def load_block(i, carry):
        at = pl.ds(pl.multiple_of(i * width, width), width)
        pltpu.make_async_copy(feat_hbm.at[:, at], feat_v.at[i], load_sem.at[0]).start()
        return carry

    lax.fori_loop(0, feat * blocks_per_dev, load_block, 0)
    owns = []
    for c in range(NC):
        start = pl.multiple_of(me * nodes + c * chunk, chunk)
        cp = pltpu.make_async_copy(feat_hbm.at[:, pl.ds(start, chunk)], xs.at[0, c, my_rows, :], own_sem.at[c])
        cp.start()
        owns.append(cp)
    for w, hbm in enumerate((ws_hbm, wn_hbm)):
        for p in range(feat):
            s = (p % 2) * (feat // 2) + ((p // 2) % mid_n) * hi_n + p // (2 * mid_n)
            pltpu.make_async_copy(
                hbm.at[pl.ds(p * rows, rows), :], w_v.at[w, pl.ds(s * rows, rows), :], load_sem.at[3 + w]
            ).start()

    pltpu.make_async_copy(feat_v, feat_v, load_sem.at[0]).wait()
    loads[0].wait()

    ones = jnp.ones((16, width), BF16)

    def group(g, acc):
        for u in range(UNROLL):
            t = g * UNROLL + u
            lhs = jnp.concatenate([feat_v[src_ref[t]], ones], axis=0)
            res = lax.dot_general(lhs, tiles_v[tile_ref[t]], (((1,), (1,)), ((), ())), preferred_element_type=F32)
            acc = acc * keep_ref[t] + res
            inv = 1.0 / jnp.maximum(acc[rows:rows + 8], 1.0)
            mean = acc[:rows].reshape(rows // 8, 8, width) * inv[None]
            pref[t] = mean.reshape(rows, width).astype(BF16)
        return acc

    lax.fori_loop(0, slots // UNROLL, group, jnp.zeros((rows + 16, width), F32))

    def mean_block(c, p, b):
        d = p * blocks_per_dev + c * per_chunk + b
        return (pref[last_ref[d]].astype(F32) * has_ref[d]).astype(BF16)

    for c in range(NC):
        def send_mean(k, carry, c=c):
            p = peer(k)
            for b in range(per_chunk):
                msend[c, p, :, b * width:(b + 1) * width] = mean_block(c, p, b)
            x_copy(1, c, k).start()
            return carry
        lax.fori_loop(0, feat - 1, send_mean, 0)
        for b in range(per_chunk):
            xs[1, c, my_rows, b * width:(b + 1) * width] = mean_block(c, me, b)

    for cp in owns:
        cp.wait()
    loads[1].wait()
    for w, hbm in enumerate((ws_hbm, wn_hbm)):
        pltpu.make_async_copy(hbm, w_v.at[w], load_sem.at[3 + w]).wait()

    def wait_x(kind, c):
        def one(k, carry):
            p = peer(k)
            pltpu.make_async_remote_copy(
                src_ref=msend.at[c, p],
                dst_ref=xs.at[kind, c, pl.ds(pl.multiple_of(slot_of(p) * rows, rows), rows), :],
                send_sem=x_send.at[kind, c, k],
                recv_sem=x_recv.at[kind, c, p],
                device_id={"feat": p},
                device_id_type=pl.DeviceIdType.MESH,
            ).wait_recv()
            return carry
        lax.fori_loop(0, feat - 1, one, 0)

    tn = (((0,), (0,)), ((), ()))
    fr = feat * rows
    half = fr // 2

    for c in range(NC):
        wait_x(0, c)

        def self_part(i, carry, c=c):
            at = pl.ds(pl.multiple_of(i * NBLK, NBLK), NBLK)
            pre_v[at, :] = lax.dot_general(xs[0, c, :, at], w_v[0], tn, preferred_element_type=F32)
            return carry

        lax.fori_loop(0, chunk // NBLK, self_part, 0)
        wait_x(1, c)

        def neigh_part(i, carry, c=c):
            at = pl.ds(pl.multiple_of(i * NBLK, NBLK), NBLK)
            pre = pre_v[at, :] + lax.dot_general(xs[1, c, :, at], w_v[1], tn, preferred_element_type=F32)
            e = jnp.exp(jnp.minimum(pre, 0.0))
            row = pl.ds(pl.multiple_of(c * chunk + i * NBLK, NBLK), NBLK)
            hid_ref[row, :] = (jnp.maximum(pre, 0.0) + (e - 1.0)).astype(BF16)
            sg_v[at, :] = (go_v[row, :].astype(F32) * e).astype(BF16)
            return carry

        lax.fori_loop(0, chunk // NBLK, neigh_part, 0)

        if c < NC - 1:
            for kind in range(2):
                def grads(i, carry, c=c, kind=kind):
                    at = pl.ds(pl.multiple_of(i * NBLK, NBLK), NBLK)
                    cols = pl.ds(kind * hid, hid)
                    g = jnp.dot(xs[kind, c, at, :], sg_v[...], preferred_element_type=F32)
                    if c > 0:
                        g = g + grad[at, cols]
                    grad[at, cols] = g
                    return carry
                lax.fori_loop(0, fr // NBLK, grads, 0)

    c = NC - 1

    def last_grads(i, kind, base):
        at = pl.ds(pl.multiple_of(base + i * NBLK, NBLK), NBLK)
        cols = pl.ds(kind * hid, hid)
        return grad[at, cols] + jnp.dot(xs[kind, c, at, :], sg_v[...], preferred_element_type=F32)

    first = []
    for kind in range(2):
        def away(i, carry, kind=kind):
            at = pl.ds(pl.multiple_of(i * NBLK, NBLK), NBLK)
            s1_send[kind, at, :] = last_grads(i, kind, (1 - core) * half)
            return carry
        lax.fori_loop(0, half // NBLK, away, 0)
        cp = pltpu.make_async_remote_copy(
            src_ref=s1_send.at[kind], dst_ref=s1_recv.at[kind],
            send_sem=s1_sems.at[0, kind], recv_sem=s1_sems.at[1, kind],
            device_id={"feat": me + 1 - 2 * core}, device_id_type=pl.DeviceIdType.MESH,
        )
        cp.start()
        first.append(cp)
    for kind in range(2):
        def home(i, carry, kind=kind):
            at = pl.ds(pl.multiple_of(core * half + i * NBLK, NBLK), NBLK)
            grad[at, pl.ds(kind * hid, hid)] = last_grads(i, kind, core * half)
            return carry
        lax.fori_loop(0, half // NBLK, home, 0)

    for kind in range(2):
        first[kind].wait_recv()
        def add1(i, carry, kind=kind):
            at = pl.ds(pl.multiple_of(core * half + i * 128, 128), 128)
            cols = pl.ds(kind * hid, hid)
            grad[at, cols] = grad[at, cols] + s1_recv[kind, pl.ds(pl.multiple_of(i * 128, 128), 128), :]
            return carry
        lax.fori_loop(0, half // 128, add1, 0)

    pending = []

    def exchange(size, mine, axis_peer, piece, send, recv, sems):
        copies = []
        for j in range(1, size):
            to = (mine + j) % size
            send[j - 1] = piece(to).astype(send.dtype)
            cp = pltpu.make_async_remote_copy(
                src_ref=send.at[j - 1], dst_ref=recv.at[j - 1],
                send_sem=sems.at[0, j - 1], recv_sem=sems.at[1, j - 1],
                device_id=axis_peer(to), device_id_type=pl.DeviceIdType.MESH,
            )
            cp.start()
            copies.append(cp)
        total = piece(mine)
        for j in range(1, size):
            copies[j - 1].wait_recv()
            total = total + recv[j - 1].astype(F32)
        pending.extend(copies)
        return total

    cb = 2 * hid // batch
    mine_rows = pl.ds(pl.multiple_of(core * half, half), half)

    def cols_of(b):
        return pl.ds(pl.multiple_of(b * cb, cb), cb)

    total2 = exchange(
        batch, mb, lambda b: {"batch": b},
        lambda b: grad[mine_rows, cols_of(b)], s2_send, s2_recv, s2_sems,
    )
    grad[mine_rows, cols_of(mb)] = total2
    span = hi_n * rows

    def rows_mid(m):
        return pl.ds(pl.multiple_of(core * half + m * span, span), span)

    total3 = exchange(
        mid_n, mid, lambda m: {"feat": hi * 2 * mid_n + m * 2 + core},
        lambda m: grad[rows_mid(m), cols_of(mb)], s3_send, s3_recv, s3_sems,
    )
    grad[rows_mid(mid), cols_of(mb)] = total3

    def rows_hi(h):
        return pl.ds(pl.multiple_of(core * half + mid * span + h * rows, rows), rows)

    total4 = exchange(
        hi_n, hi, lambda h: {"feat": h * 2 * mid_n + mid * 2 + core},
        lambda h: grad[rows_hi(h), cols_of(mb)], s4_send, s4_recv, s4_sems,
    )
    s5_send[...] = total4
    gather = []
    for j in range(1, batch):
        cp = pltpu.make_async_remote_copy(
            src_ref=s5_send, dst_ref=s5_recv.at[j - 1],
            send_sem=s5_sems.at[0, j - 1], recv_sem=s5_sems.at[1, j - 1],
            device_id={"batch": (mb + j) % batch}, device_id_type=pl.DeviceIdType.MESH,
        )
        cp.start()
        gather.append(cp)
    gw_ref[:, cols_of(mb)] = total4
    for j in range(1, batch):
        gather[j - 1].wait_recv()
        gw_ref[:, cols_of((mb + batch - j) % batch)] = s5_recv[j - 1]

    for cp in first + pending + gather:
        cp.wait_send()
    for kind in range(2):
        for c in range(NC):
            def sent(k, carry, kind=kind, c=c):
                x_copy(kind, c, k).wait_send()
                return carry
            lax.fori_loop(0, feat - 1, sent, 0)


def body(feat, batch, features, tile_values, tile_blocks, tile_count, w_self, w_neigh, grad_out):
    rows, node_total = features.shape[1:]
    slots, width = tile_values.shape[1], tile_values.shape[-1]
    nodes, hid = grad_out.shape[1:]
    nb = node_total // width
    hi_n = 4
    mid_n = feat // (2 * hi_n)
    t = jnp.arange(slots, dtype=jnp.int32)
    key = jnp.where(t < tile_count[0], tile_blocks[0, 0], nb)
    full = key * slots + t
    rank = jnp.sum((full[None, :] < full[:, None]).astype(jnp.int32), axis=1)
    hit = rank[None, :] == t[:, None]
    tile_order = jnp.sum(jnp.where(hit, t[None, :], 0), axis=1)
    src_order = jnp.sum(jnp.where(hit, tile_blocks[0, 1][None, :], 0), axis=1)
    keys = jnp.sum(jnp.where(hit, key[None, :], 0), axis=1)
    before = jnp.concatenate([jnp.full((1,), -1, jnp.int32), keys[:-1]])
    keep = (keys == before).astype(F32)
    d = jnp.arange(nb, dtype=jnp.int32)
    upto = jnp.sum((key[None, :] <= d[:, None]).astype(jnp.int32), axis=1)
    has = jnp.max((key[None, :] == d[:, None]).astype(F32), axis=1)
    last = jnp.maximum(upto - 1, 0)

    dims = (feat, batch, hi_n, mid_n, rows, nodes, width, slots, hid)
    fr = feat * rows
    chunk = nodes // NC
    cb = 2 * hid // batch
    span = hi_n * rows
    s4_type = BF16 if batch == 2 else F32
    dma = pltpu.SemaphoreType.DMA
    any_spec = pl.BlockSpec(memory_space=pl.ANY)
    smem = pl.BlockSpec(memory_space=pltpu.SMEM)
    vmem = pl.BlockSpec(memory_space=pltpu.VMEM)
    hidden, grad_w = pl.pallas_call(
        functools.partial(kernel, dims),
        out_shape=(
            jax.ShapeDtypeStruct((nodes, hid), BF16),
            jax.ShapeDtypeStruct((rows, 2 * hid), F32),
        ),
        in_specs=[smem] * 5 + [any_spec] * 5,
        out_specs=(vmem, vmem),
        scratch_shapes=[
            pltpu.VMEM((nb, rows, width), BF16),
            pltpu.VMEM((slots, width, width), BF16),
            pltpu.VMEM((2, fr, hid), BF16),
            pltpu.VMEM((nodes, hid), BF16),
            pltpu.VMEM((slots, rows, width), BF16),
            pltpu.VMEM((NC, feat, rows, chunk), BF16),
            pltpu.VMEM((2, NC, fr, chunk), BF16),
            pltpu.VMEM((chunk, hid), F32),
            pltpu.VMEM((chunk, hid), BF16),
            pltpu.VMEM((fr, 2 * hid), F32),
            pltpu.VMEM((2, fr // 2, hid), F32),
            pltpu.VMEM((2, fr // 2, hid), F32),
            pltpu.VMEM((batch - 1, fr // 2, cb), BF16),
            pltpu.VMEM((batch - 1, fr // 2, cb), BF16),
            pltpu.VMEM((mid_n - 1, span, cb), F32),
            pltpu.VMEM((mid_n - 1, span, cb), F32),
            pltpu.VMEM((hi_n - 1, rows, cb), s4_type),
            pltpu.VMEM((hi_n - 1, rows, cb), s4_type),
            pltpu.VMEM((rows, cb), F32),
            pltpu.VMEM((batch - 1, rows, cb), F32),
            dma((5,)),
            dma((NC,)),
            dma((2, NC, feat - 1)),
            dma((2, NC, feat)),
            dma((2, 2)),
            dma((2, batch - 1)),
            dma((2, mid_n - 1)),
            dma((2, hi_n - 1)),
            dma((2, batch - 1)),
        ],
        compiler_params=pltpu.CompilerParams(
            collective_id=0, has_side_effects=True, vmem_limit_bytes=58 * 1024 * 1024
        ),
    )(tile_order, src_order, keep, last, has, features[0], tile_values[0], w_self, w_neigh, grad_out[0])
    return hidden[None], grad_w.reshape(rows, 2, hid)


def solution(mesh):
    in_specs = (
        P("batch", "feat", None),
        P("batch", None, None, None),
        P("batch", None, None),
        P("batch"),
        P(),
        P(),
        P("batch", "feat", None),
    )
    out_specs = (P("batch", "feat", None), P("feat", None, None))
    fn = functools.partial(body, mesh.shape["feat"], mesh.shape["batch"])
    return jax.shard_map(fn, mesh=mesh, in_specs=in_specs, out_specs=out_specs, check_vma=False)
```

```python
import functools

import jax
import jax.numpy as jnp
from jax import lax
from jax.experimental import pallas as pl
from jax.experimental.pallas import tpu as pltpu
from jax.sharding import PartitionSpec as P

F32 = jnp.float32
BF16 = jnp.bfloat16
NC = 2
UNROLL = 8
NBLK = 256


def kernel(
    dims,
    tile_ref, src_ref, keep_ref, last_ref, has_ref, feat_hbm, tiles_hbm, ws_hbm, wn_hbm, go_hbm,
    hid_ref, gw_ref,
    feat_v, tiles_v, w_v, go_v, pref, msend, xs, pre_v, sg_v, grad,
    s1_send, s1_recv, s2_send, s2_recv, s3_send, s3_recv, s4_send, s4_recv, s5_send, s5_recv, s6_send, s6_recv, s7_send, s7_recv,
    load_sem, own_sem, x_send, x_recv, s1_sems, s2_sems, s3_sems, s4_sems, s5_sems, s6_sems, s7_sems,
):
    feat, batch, hi_n, mid_n, rows, nodes, width, slots, hid = dims
    chunk = nodes // NC
    per_chunk = chunk // width
    blocks_per_dev = nodes // width
    me = lax.axis_index("feat")
    mb = lax.axis_index("batch")
    hi = me // (2 * mid_n)
    mid = (me // 2) % mid_n
    core = me % 2

    hf = hi_n // 2

    def slot_of(p):
        h = p // (2 * mid_n)
        return (p % 2) * (feat // 2) + (h // hf) * mid_n * hf + ((p // 2) % mid_n) * hf + h % hf

    my_rows = pl.ds(pl.multiple_of(slot_of(me) * rows, rows), rows)

    def peer(k):
        return (me + 1 + (k + feat // 2 - 1) % (feat - 1)) % feat

    loads = [
        pltpu.make_async_copy(tiles_hbm, tiles_v, load_sem.at[1]),
        pltpu.make_async_copy(go_hbm, go_v, load_sem.at[2]),
    ]
    for cp in loads:
        cp.start()

    barrier = pltpu.get_barrier_semaphore()

    def greet(k, carry):
        pl.semaphore_signal(barrier, inc=1, device_id={"feat": peer(k)}, device_id_type=pl.DeviceIdType.MESH)
        return carry

    lax.fori_loop(0, feat - 1, greet, 0)
    for j in range(1, batch):
        pl.semaphore_signal(
            barrier, inc=1, device_id={"batch": (mb + j) % batch}, device_id_type=pl.DeviceIdType.MESH
        )
    pl.semaphore_wait(barrier, feat - 1 + batch - 1)

    def x_copy(kind, c, k):
        p = peer(k)
        if kind == 0:
            start = pl.multiple_of(p * nodes + c * chunk, chunk)
            src = feat_hbm.at[:, pl.ds(start, chunk)]
        else:
            src = msend.at[c, p]
        return pltpu.make_async_remote_copy(
            src_ref=src,
            dst_ref=xs.at[kind, c, my_rows, :],
            send_sem=x_send.at[kind, c, k],
            recv_sem=x_recv.at[kind, c, me],
            device_id={"feat": p},
            device_id_type=pl.DeviceIdType.MESH,
        )

    for c in range(NC):
        def send_feat(k, carry, c=c):
            x_copy(0, c, k).start()
            return carry
        lax.fori_loop(0, feat - 1, send_feat, 0)

    def load_block(i, carry):
        at = pl.ds(pl.multiple_of(i * width, width), width)
        pltpu.make_async_copy(feat_hbm.at[:, at], feat_v.at[i], load_sem.at[0]).start()
        return carry

    lax.fori_loop(0, feat * blocks_per_dev, load_block, 0)
    owns = []
    for c in range(NC):
        start = pl.multiple_of(me * nodes + c * chunk, chunk)
        cp = pltpu.make_async_copy(feat_hbm.at[:, pl.ds(start, chunk)], xs.at[0, c, my_rows, :], own_sem.at[c])
        cp.start()
        owns.append(cp)
    for w, hbm in enumerate((ws_hbm, wn_hbm)):
        for p in range(feat):
            s = slot_of(p)
            pltpu.make_async_copy(
                hbm.at[pl.ds(p * rows, rows), :], w_v.at[w, pl.ds(s * rows, rows), :], load_sem.at[3 + w]
            ).start()

    pltpu.make_async_copy(feat_v, feat_v, load_sem.at[0]).wait()
    loads[0].wait()

    ones = jnp.ones((16, width), BF16)

    def group(g, acc):
        for u in range(UNROLL):
            t = g * UNROLL + u
            lhs = jnp.concatenate([feat_v[src_ref[t]], ones], axis=0)
            res = lax.dot_general(lhs, tiles_v[tile_ref[t]], (((1,), (1,)), ((), ())), preferred_element_type=F32)
            acc = acc * keep_ref[t] + res
            inv = 1.0 / jnp.maximum(acc[rows:rows + 8], 1.0)
            mean = acc[:rows].reshape(rows // 8, 8, width) * inv[None]
            pref[t] = mean.reshape(rows, width).astype(BF16)
        return acc

    lax.fori_loop(0, slots // UNROLL, group, jnp.zeros((rows + 16, width), F32))

    def mean_block(c, p, b):
        d = p * blocks_per_dev + c * per_chunk + b
        return (pref[last_ref[d]].astype(F32) * has_ref[d]).astype(BF16)

    for c in range(NC):
        def send_mean(k, carry, c=c):
            p = peer(k)
            for b in range(per_chunk):
                msend[c, p, :, b * width:(b + 1) * width] = mean_block(c, p, b)
            x_copy(1, c, k).start()
            return carry
        lax.fori_loop(0, feat - 1, send_mean, 0)
        for b in range(per_chunk):
            xs[1, c, my_rows, b * width:(b + 1) * width] = mean_block(c, me, b)

    for cp in owns:
        cp.wait()
    loads[1].wait()
    for w, hbm in enumerate((ws_hbm, wn_hbm)):
        pltpu.make_async_copy(hbm, w_v.at[w], load_sem.at[3 + w]).wait()

    def wait_x(kind, c):
        def one(k, carry):
            p = peer(k)
            pltpu.make_async_remote_copy(
                src_ref=msend.at[c, p],
                dst_ref=xs.at[kind, c, pl.ds(pl.multiple_of(slot_of(p) * rows, rows), rows), :],
                send_sem=x_send.at[kind, c, k],
                recv_sem=x_recv.at[kind, c, p],
                device_id={"feat": p},
                device_id_type=pl.DeviceIdType.MESH,
            ).wait_recv()
            return carry
        lax.fori_loop(0, feat - 1, one, 0)

    tn = (((0,), (0,)), ((), ()))
    fr = feat * rows
    half = fr // 2

    for c in range(NC):
        wait_x(0, c)

        def self_part(i, carry, c=c):
            at = pl.ds(pl.multiple_of(i * NBLK, NBLK), NBLK)
            pre_v[at, :] = lax.dot_general(xs[0, c, :, at], w_v[0], tn, preferred_element_type=F32)
            return carry

        lax.fori_loop(0, chunk // NBLK, self_part, 0)
        wait_x(1, c)

        def neigh_part(i, carry, c=c):
            at = pl.ds(pl.multiple_of(i * NBLK, NBLK), NBLK)
            pre = pre_v[at, :] + lax.dot_general(xs[1, c, :, at], w_v[1], tn, preferred_element_type=F32)
            e = jnp.exp(jnp.minimum(pre, 0.0))
            row = pl.ds(pl.multiple_of(c * chunk + i * NBLK, NBLK), NBLK)
            hid_ref[row, :] = (jnp.maximum(pre, 0.0) + (e - 1.0)).astype(BF16)
            sg_v[at, :] = (go_v[row, :].astype(F32) * e).astype(BF16)
            return carry

        lax.fori_loop(0, chunk // NBLK, neigh_part, 0)

        if c < NC - 1:
            for kind in range(2):
                def grads(i, carry, c=c, kind=kind):
                    at = pl.ds(pl.multiple_of(i * NBLK, NBLK), NBLK)
                    cols = pl.ds(kind * hid, hid)
                    g = jnp.dot(xs[kind, c, at, :], sg_v[...], preferred_element_type=F32)
                    if c > 0:
                        g = g + grad[at, cols]
                    grad[at, cols] = g
                    return carry
                lax.fori_loop(0, fr // NBLK, grads, 0)

    c = NC - 1

    def last_grads(i, kind, base):
        at = pl.ds(pl.multiple_of(base + i * NBLK, NBLK), NBLK)
        cols = pl.ds(kind * hid, hid)
        return grad[at, cols] + jnp.dot(xs[kind, c, at, :], sg_v[...], preferred_element_type=F32)

    first = []
    for kind in range(2):
        def away(i, carry, kind=kind):
            at = pl.ds(pl.multiple_of(i * NBLK, NBLK), NBLK)
            s1_send[kind, at, :] = last_grads(i, kind, (1 - core) * half)
            return carry
        lax.fori_loop(0, half // NBLK, away, 0)
        cp = pltpu.make_async_remote_copy(
            src_ref=s1_send.at[kind], dst_ref=s1_recv.at[kind],
            send_sem=s1_sems.at[0, kind], recv_sem=s1_sems.at[1, kind],
            device_id={"feat": me + 1 - 2 * core}, device_id_type=pl.DeviceIdType.MESH,
        )
        cp.start()
        first.append(cp)
    for kind in range(2):
        def home(i, carry, kind=kind):
            at = pl.ds(pl.multiple_of(core * half + i * NBLK, NBLK), NBLK)
            grad[at, pl.ds(kind * hid, hid)] = last_grads(i, kind, core * half)
            return carry
        lax.fori_loop(0, half // NBLK, home, 0)

    for kind in range(2):
        first[kind].wait_recv()
        def add1(i, carry, kind=kind):
            at = pl.ds(pl.multiple_of(core * half + i * 128, 128), 128)
            cols = pl.ds(kind * hid, hid)
            grad[at, cols] = grad[at, cols] + s1_recv[kind, pl.ds(pl.multiple_of(i * 128, 128), 128), :]
            return carry
        lax.fori_loop(0, half // 128, add1, 0)

    pending = []

    cb = 2 * hid // batch
    quarter = half // 2
    part = hf * rows

    def cols_of(b):
        return pl.ds(pl.multiple_of(b * cb, cb), cb)

    def flow_rows(f):
        return pl.ds(pl.multiple_of(core * half + f * quarter, quarter), quarter)

    def mid_rows(f, m):
        return pl.ds(pl.multiple_of(core * half + f * quarter + m * part, part), part)

    def hi_rows(h):
        return pl.ds(
            pl.multiple_of(core * half + (h // hf) * quarter + mid * part + (h % hf) * rows, rows), rows
        )

    every = pl.ds(0, 2 * hid)

    def to_batch(b):
        return {"batch": b}

    def to_mid(m):
        return {"feat": hi * 2 * mid_n + m * 2 + core}

    def to_hi(h):
        return {"feat": h * 2 * mid_n + mid * 2 + core}

    def send_parts(size, mine, place, where, send, recv, sems):
        copies = []
        for j in range(1, size):
            to = (mine + j) % size
            at, cols = where(to)
            send[j - 1] = grad[at, cols].astype(send.dtype)
            cp = pltpu.make_async_remote_copy(
                src_ref=send.at[j - 1], dst_ref=recv.at[j - 1],
                send_sem=sems.at[0, j - 1], recv_sem=sems.at[1, j - 1],
                device_id=place(to), device_id_type=pl.DeviceIdType.MESH,
            )
            cp.start()
            copies.append(cp)
        pending.extend(copies)
        return copies

    def add_parts(copies, where, recv):
        at, cols = where
        total = grad[at, cols]
        for j, cp in enumerate(copies):
            cp.wait_recv()
            total = total + recv[j].astype(F32)
        grad[at, cols] = total
        return total

    wb0 = lambda b: (flow_rows(0), cols_of(b))
    wm1 = lambda m: (mid_rows(1, m), every)
    wm0 = lambda m: (mid_rows(0, m), cols_of(mb))
    wb1 = lambda b: (mid_rows(1, mid), cols_of(b))
    first_b = send_parts(batch, mb, to_batch, wb0, s2_send, s2_recv, s2_sems)
    first_m = send_parts(mid_n, mid, to_mid, wm1, s3_send, s3_recv, s3_sems)
    add_parts(first_b, wb0(mb), s2_recv)
    second_m = send_parts(mid_n, mid, to_mid, wm0, s6_send, s6_recv, s6_sems)
    add_parts(first_m, wm1(mid), s3_recv)
    second_b = send_parts(batch, mb, to_batch, wb1, s7_send, s7_recv, s7_sems)
    add_parts(second_m, wm0(mid), s6_recv)
    add_parts(second_b, wb1(mb), s7_recv)
    wh = lambda h: (hi_rows(h), cols_of(mb))
    across = send_parts(hi_n, hi, to_hi, wh, s4_send, s4_recv, s4_sems)
    total4 = add_parts(across, wh(hi), s4_recv)
    s5_send[...] = total4
    gather = []
    for j in range(1, batch):
        cp = pltpu.make_async_remote_copy(
            src_ref=s5_send, dst_ref=s5_recv.at[j - 1],
            send_sem=s5_sems.at[0, j - 1], recv_sem=s5_sems.at[1, j - 1],
            device_id={"batch": (mb + j) % batch}, device_id_type=pl.DeviceIdType.MESH,
        )
        cp.start()
        gather.append(cp)
    gw_ref[:, cols_of(mb)] = total4
    for j in range(1, batch):
        gather[j - 1].wait_recv()
        gw_ref[:, cols_of((mb + batch - j) % batch)] = s5_recv[j - 1]

    for cp in first + pending + gather:
        cp.wait_send()
    for kind in range(2):
        for c in range(NC):
            def sent(k, carry, kind=kind, c=c):
                x_copy(kind, c, k).wait_send()
                return carry
            lax.fori_loop(0, feat - 1, sent, 0)


def body(feat, batch, features, tile_values, tile_blocks, tile_count, w_self, w_neigh, grad_out):
    rows, node_total = features.shape[1:]
    slots, width = tile_values.shape[1], tile_values.shape[-1]
    nodes, hid = grad_out.shape[1:]
    nb = node_total // width
    hi_n = 4
    mid_n = feat // (2 * hi_n)
    t = jnp.arange(slots, dtype=jnp.int32)
    key = jnp.where(t < tile_count[0], tile_blocks[0, 0], nb)
    full = key * slots + t
    rank = jnp.sum((full[None, :] < full[:, None]).astype(jnp.int32), axis=1)
    hit = rank[None, :] == t[:, None]
    tile_order = jnp.sum(jnp.where(hit, t[None, :], 0), axis=1)
    src_order = jnp.sum(jnp.where(hit, tile_blocks[0, 1][None, :], 0), axis=1)
    keys = jnp.sum(jnp.where(hit, key[None, :], 0), axis=1)
    before = jnp.concatenate([jnp.full((1,), -1, jnp.int32), keys[:-1]])
    keep = (keys == before).astype(F32)
    d = jnp.arange(nb, dtype=jnp.int32)
    upto = jnp.sum((key[None, :] <= d[:, None]).astype(jnp.int32), axis=1)
    has = jnp.max((key[None, :] == d[:, None]).astype(F32), axis=1)
    last = jnp.maximum(upto - 1, 0)

    dims = (feat, batch, hi_n, mid_n, rows, nodes, width, slots, hid)
    fr = feat * rows
    chunk = nodes // NC
    cb = 2 * hid // batch
    span = hi_n * rows
    s4_type = BF16 if batch == 2 else F32
    dma = pltpu.SemaphoreType.DMA
    any_spec = pl.BlockSpec(memory_space=pl.ANY)
    smem = pl.BlockSpec(memory_space=pltpu.SMEM)
    vmem = pl.BlockSpec(memory_space=pltpu.VMEM)
    hidden, grad_w = pl.pallas_call(
        functools.partial(kernel, dims),
        out_shape=(
            jax.ShapeDtypeStruct((nodes, hid), BF16),
            jax.ShapeDtypeStruct((rows, 2 * hid), F32),
        ),
        in_specs=[smem] * 5 + [any_spec] * 5,
        out_specs=(vmem, vmem),
        scratch_shapes=[
            pltpu.VMEM((nb, rows, width), BF16),
            pltpu.VMEM((slots, width, width), BF16),
            pltpu.VMEM((2, fr, hid), BF16),
            pltpu.VMEM((nodes, hid), BF16),
            pltpu.VMEM((slots, rows, width), BF16),
            pltpu.VMEM((NC, feat, rows, chunk), BF16),
            pltpu.VMEM((2, NC, fr, chunk), BF16),
            pltpu.VMEM((chunk, hid), F32),
            pltpu.VMEM((chunk, hid), BF16),
            pltpu.VMEM((fr, 2 * hid), F32),
            pltpu.VMEM((2, fr // 2, hid), F32),
            pltpu.VMEM((2, fr // 2, hid), F32),
            pltpu.VMEM((batch - 1, fr // 4, cb), BF16),
            pltpu.VMEM((batch - 1, fr // 4, cb), BF16),
            pltpu.VMEM((mid_n - 1, span // 2, 2 * hid), BF16),
            pltpu.VMEM((mid_n - 1, span // 2, 2 * hid), BF16),
            pltpu.VMEM((hi_n - 1, rows, cb), s4_type),
            pltpu.VMEM((hi_n - 1, rows, cb), s4_type),
            pltpu.VMEM((rows, cb), F32),
            pltpu.VMEM((batch - 1, rows, cb), F32),
            pltpu.VMEM((mid_n - 1, span // 2, cb), F32),
            pltpu.VMEM((mid_n - 1, span // 2, cb), F32),
            pltpu.VMEM((batch - 1, span // 2, cb), F32),
            pltpu.VMEM((batch - 1, span // 2, cb), F32),
            dma((5,)),
            dma((NC,)),
            dma((2, NC, feat - 1)),
            dma((2, NC, feat)),
            dma((2, 2)),
            dma((2, batch - 1)),
            dma((2, mid_n - 1)),
            dma((2, hi_n - 1)),
            dma((2, batch - 1)),
            dma((2, mid_n - 1)),
            dma((2, batch - 1)),
        ],
        compiler_params=pltpu.CompilerParams(
            collective_id=0, has_side_effects=True, vmem_limit_bytes=58 * 1024 * 1024
        ),
    )(tile_order, src_order, keep, last, has, features[0], tile_values[0], w_self, w_neigh, grad_out[0])
    return hidden[None], grad_w.reshape(rows, 2, hid)


def solution(mesh):
    in_specs = (
        P("batch", "feat", None),
        P("batch", None, None, None),
        P("batch", None, None),
        P("batch"),
        P(),
        P(),
        P("batch", "feat", None),
    )
    out_specs = (P("batch", "feat", None), P("feat", None, None))
    fn = functools.partial(body, mesh.shape["feat"], mesh.shape["batch"])
    return jax.shard_map(fn, mesh=mesh, in_specs=in_specs, out_specs=out_specs, check_vma=False)
```

```python
import functools

import jax
import jax.numpy as jnp
from jax import lax
from jax.experimental import pallas as pl
from jax.experimental.pallas import tpu as pltpu
from jax.sharding import PartitionSpec as P

F32 = jnp.float32
BF16 = jnp.bfloat16
NC = 2
UNROLL = 8
NBLK = 256


def kernel(
    dims,
    tile_ref, src_ref, key_ref, last_ref, feat_hbm, tiles_hbm, ws_hbm, wn_hbm, go_hbm,
    hid_ref, gw_ref,
    feat_v, tiles_v, w_v, go_v, pref, msend, xs, pre_v, sg_v, grad,
    s1_send, s1_recv, s2_send, s2_recv, s3_send, s3_recv, s4_send, s4_recv, s5_send, s5_recv, s6_send, s6_recv, s7_send, s7_recv, gw_v,
    load_sem, own_sem, x_send, x_recv, s1_sems, s2_sems, s3_sems, s4_sems, s5_sems, s6_sems, s7_sems,
):
    feat, batch, hi_n, mid_n, rows, nodes, width, slots, hid = dims
    chunk = nodes // NC
    per_chunk = chunk // width
    blocks_per_dev = nodes // width
    me = lax.axis_index("feat")
    mb = lax.axis_index("batch")
    hi = me // (2 * mid_n)
    mid = (me // 2) % mid_n
    core = me % 2

    hf = hi_n // 2

    def slot_of(p):
        h = p // (2 * mid_n)
        return (p % 2) * (feat // 2) + (h // hf) * mid_n * hf + ((p // 2) % mid_n) * hf + h % hf

    my_rows = pl.ds(pl.multiple_of(slot_of(me) * rows, rows), rows)

    def peer(k):
        return (me + 1 + (k + feat // 2 - 1) % (feat - 1)) % feat

    loads = [
        pltpu.make_async_copy(tiles_hbm, tiles_v, load_sem.at[1]),
        pltpu.make_async_copy(go_hbm, go_v, load_sem.at[2]),
    ]
    for cp in loads:
        cp.start()

    barrier = pltpu.get_barrier_semaphore()

    def greet(k, carry):
        pl.semaphore_signal(barrier, inc=1, device_id={"feat": peer(k)}, device_id_type=pl.DeviceIdType.MESH)
        return carry

    lax.fori_loop(0, feat - 1, greet, 0)
    for j in range(1, batch):
        pl.semaphore_signal(
            barrier, inc=1, device_id={"batch": (mb + j) % batch}, device_id_type=pl.DeviceIdType.MESH
        )
    pl.semaphore_wait(barrier, feat - 1 + batch - 1)

    def x_copy(kind, c, k):
        p = peer(k)
        if kind == 0:
            start = pl.multiple_of(p * nodes + c * chunk, chunk)
            src = feat_hbm.at[:, pl.ds(start, chunk)]
        else:
            src = msend.at[c, p]
        return pltpu.make_async_remote_copy(
            src_ref=src,
            dst_ref=xs.at[kind, c, my_rows, :],
            send_sem=x_send.at[kind, c, k],
            recv_sem=x_recv.at[kind, c, me],
            device_id={"feat": p},
            device_id_type=pl.DeviceIdType.MESH,
        )

    for c in range(NC):
        def send_feat(k, carry, c=c):
            x_copy(0, c, k).start()
            return carry
        lax.fori_loop(0, feat - 1, send_feat, 0)

    def load_block(i, carry):
        at = pl.ds(pl.multiple_of(i * width, width), width)
        pltpu.make_async_copy(feat_hbm.at[:, at], feat_v.at[i], load_sem.at[0]).start()
        return carry

    lax.fori_loop(0, feat * blocks_per_dev, load_block, 0)
    owns = []
    for c in range(NC):
        start = pl.multiple_of(me * nodes + c * chunk, chunk)
        cp = pltpu.make_async_copy(feat_hbm.at[:, pl.ds(start, chunk)], xs.at[0, c, my_rows, :], own_sem.at[c])
        cp.start()
        owns.append(cp)
    for w, hbm in enumerate((ws_hbm, wn_hbm)):
        for p in range(feat):
            s = slot_of(p)
            pltpu.make_async_copy(
                hbm.at[pl.ds(p * rows, rows), :], w_v.at[w, pl.ds(s * rows, rows), :], load_sem.at[3 + w]
            ).start()

    pltpu.make_async_copy(feat_v, feat_v, load_sem.at[0]).wait()
    loads[0].wait()

    ones = jnp.ones((16, width), BF16)

    pref[slots] = jnp.zeros((rows, width), BF16)

    def group(g, acc):
        for u in range(UNROLL):
            t = g * UNROLL + u
            lhs = jnp.concatenate([feat_v[src_ref[t]], ones], axis=0)
            res = lax.dot_general(lhs, tiles_v[tile_ref[t]], (((1,), (1,)), ((), ())), preferred_element_type=F32)
            same = 1 - jnp.minimum(key_ref[t] - key_ref[jnp.maximum(t - 1, 0)], 1)
            acc = acc * same.astype(F32) + res
            inv = 1.0 / jnp.maximum(acc[rows:rows + 8], 1.0)
            mean = acc[:rows].reshape(rows // 8, 8, width) * inv[None]
            pref[t] = mean.reshape(rows, width).astype(BF16)
        return acc

    lax.fori_loop(0, slots // UNROLL, group, jnp.zeros((rows + 16, width), F32))

    def mean_block(c, p, b):
        d = p * blocks_per_dev + c * per_chunk + b
        return pref[last_ref[d]]

    for c in range(NC):
        def send_mean(k, carry, c=c):
            p = peer(k)
            for b in range(per_chunk):
                msend[c, p, :, b * width:(b + 1) * width] = mean_block(c, p, b)
            x_copy(1, c, k).start()
            return carry
        lax.fori_loop(0, feat - 1, send_mean, 0)
        for b in range(per_chunk):
            xs[1, c, my_rows, b * width:(b + 1) * width] = mean_block(c, me, b)

    for cp in owns:
        cp.wait()
    loads[1].wait()
    for w, hbm in enumerate((ws_hbm, wn_hbm)):
        pltpu.make_async_copy(hbm, w_v.at[w], load_sem.at[3 + w]).wait()

    def wait_x(kind, c):
        def one(k, carry):
            p = peer(k)
            pltpu.make_async_remote_copy(
                src_ref=msend.at[c, p],
                dst_ref=xs.at[kind, c, pl.ds(pl.multiple_of(slot_of(p) * rows, rows), rows), :],
                send_sem=x_send.at[kind, c, k],
                recv_sem=x_recv.at[kind, c, p],
                device_id={"feat": p},
                device_id_type=pl.DeviceIdType.MESH,
            ).wait_recv()
            return carry
        lax.fori_loop(0, feat - 1, one, 0)

    tn = (((0,), (0,)), ((), ()))
    fr = feat * rows
    half = fr // 2

    for c in range(NC):
        wait_x(0, c)

        def self_part(i, carry, c=c):
            at = pl.ds(pl.multiple_of(i * NBLK, NBLK), NBLK)
            pre_v[at, :] = lax.dot_general(xs[0, c, :, at], w_v[0], tn, preferred_element_type=F32)
            return carry

        lax.fori_loop(0, chunk // NBLK, self_part, 0)
        wait_x(1, c)

        def neigh_part(i, carry, c=c):
            at = pl.ds(pl.multiple_of(i * NBLK, NBLK), NBLK)
            pre = pre_v[at, :] + lax.dot_general(xs[1, c, :, at], w_v[1], tn, preferred_element_type=F32)
            e = jnp.exp(jnp.minimum(pre, 0.0))
            row = pl.ds(pl.multiple_of(c * chunk + i * NBLK, NBLK), NBLK)
            hid_ref[row, :] = (jnp.maximum(pre, 0.0) + (e - 1.0)).astype(BF16)
            sg_v[at, :] = (go_v[row, :].astype(F32) * e).astype(BF16)
            return carry

        lax.fori_loop(0, chunk // NBLK, neigh_part, 0)

        if c < NC - 1:
            for kind in range(2):
                def grads(i, carry, c=c, kind=kind):
                    at = pl.ds(pl.multiple_of(i * NBLK, NBLK), NBLK)
                    cols = pl.ds(kind * hid, hid)
                    g = jnp.dot(xs[kind, c, at, :], sg_v[...], preferred_element_type=F32)
                    if c > 0:
                        g = g + grad[at, cols]
                    grad[at, cols] = g
                    return carry
                lax.fori_loop(0, fr // NBLK, grads, 0)

    c = NC - 1

    def last_grads(base, i):
        at = pl.ds(pl.multiple_of(base + (i // 2) * NBLK, NBLK), NBLK)
        cols = pl.ds(pl.multiple_of((i % 2) * hid, hid), hid)
        return at, cols, grad[at, cols] + jnp.dot(xs[i % 2, c, at, :], sg_v[...], preferred_element_type=F32)

    quarter = half // 2
    steps = 2 * quarter // NBLK
    first = []
    for f in range(2):
        def away(i, carry, f=f):
            _, cols, g = last_grads((1 - core) * half + f * quarter, i)
            s1_send[f, pl.ds(pl.multiple_of((i // 2) * NBLK, NBLK), NBLK), cols] = g
            return carry
        lax.fori_loop(0, steps, away, 0)
        cp = pltpu.make_async_remote_copy(
            src_ref=s1_send.at[f], dst_ref=s1_recv.at[f],
            send_sem=s1_sems.at[0, f], recv_sem=s1_sems.at[1, f],
            device_id={"feat": me + 1 - 2 * core}, device_id_type=pl.DeviceIdType.MESH,
        )
        cp.start()
        first.append(cp)

    def home(i, carry):
        at, cols, g = last_grads(core * half, i)
        grad[at, cols] = g
        return carry

    lax.fori_loop(0, 2 * steps, home, 0)

    def add_core(f):
        first[f].wait_recv()

        def add1(i, carry):
            at = pl.ds(pl.multiple_of(core * half + f * quarter + i * 64, 64), 64)
            grad[at, :] = grad[at, :] + s1_recv[f, pl.ds(pl.multiple_of(i * 64, 64), 64), :]
            return carry

        lax.fori_loop(0, quarter // 64, add1, 0)

    pending = []

    cb = 2 * hid // batch
    part = hf * rows

    def cols_of(b):
        return pl.ds(pl.multiple_of(b * cb, cb), cb)

    def flow_rows(f):
        return pl.ds(pl.multiple_of(core * half + f * quarter, quarter), quarter)

    def mid_rows(f, m):
        return pl.ds(pl.multiple_of(core * half + f * quarter + m * part, part), part)

    def hi_rows(h):
        return pl.ds(
            pl.multiple_of(core * half + (h // hf) * quarter + mid * part + (h % hf) * rows, rows), rows
        )

    every = pl.ds(0, 2 * hid)

    def to_batch(b):
        return {"batch": b}

    def to_mid(m):
        return {"feat": hi * 2 * mid_n + m * 2 + core}

    def to_hi(h):
        return {"feat": h * 2 * mid_n + mid * 2 + core}

    def send_parts(size, mine, place, where, send, recv, sems):
        copies = []
        for j in range(1, size):
            to = (mine + j) % size
            at, cols = where(to)
            send[j - 1] = grad[at, cols].astype(send.dtype)
            cp = pltpu.make_async_remote_copy(
                src_ref=send.at[j - 1], dst_ref=recv.at[j - 1],
                send_sem=sems.at[0, j - 1], recv_sem=sems.at[1, j - 1],
                device_id=place(to), device_id_type=pl.DeviceIdType.MESH,
            )
            cp.start()
            copies.append(cp)
        pending.extend(copies)
        return copies

    def add_parts(copies, where, recv):
        at, cols = where
        total = grad[at, cols]
        for j, cp in enumerate(copies):
            cp.wait_recv()
            total = total + recv[j].astype(F32)
        grad[at, cols] = total
        return total

    wb0 = lambda b: (flow_rows(0), cols_of(b))
    wm1 = lambda m: (mid_rows(1, m), every)
    wm0 = lambda m: (mid_rows(0, m), cols_of(mb))
    wb1 = lambda b: (mid_rows(1, mid), cols_of(b))
    add_core(0)
    first_b = send_parts(batch, mb, to_batch, wb0, s2_send, s2_recv, s2_sems)
    add_core(1)
    first_m = send_parts(mid_n, mid, to_mid, wm1, s3_send, s3_recv, s3_sems)
    add_parts(first_b, wb0(mb), s2_recv)
    second_m = send_parts(mid_n, mid, to_mid, wm0, s6_send, s6_recv, s6_sems)
    add_parts(first_m, wm1(mid), s3_recv)
    second_b = send_parts(batch, mb, to_batch, wb1, s7_send, s7_recv, s7_sems)
    add_parts(second_m, wm0(mid), s6_recv)
    add_parts(second_b, wb1(mb), s7_recv)
    wh = lambda h: (hi_rows(h), cols_of(mb))
    across = send_parts(hi_n, hi, to_hi, wh, s4_send, s4_recv, s4_sems)
    total4 = add_parts(across, wh(hi), s4_recv)
    s5_send[...] = total4
    gather = []
    for j in range(1, batch):
        cp = pltpu.make_async_remote_copy(
            src_ref=s5_send, dst_ref=s5_recv.at[j - 1],
            send_sem=s5_sems.at[0, j - 1], recv_sem=s5_sems.at[1, j - 1],
            device_id={"batch": (mb + j) % batch}, device_id_type=pl.DeviceIdType.MESH,
        )
        cp.start()
        gather.append(cp)
    gw_v[:, cols_of(mb)] = total4
    for j in range(1, batch):
        gather[j - 1].wait_recv()
        gw_v[:, cols_of((mb + batch - j) % batch)] = s5_recv[j - 1]
    for kind in range(2):
        gw_ref[:, kind, :] = gw_v[:, kind * hid:(kind + 1) * hid]

    for cp in first + pending + gather:
        cp.wait_send()
    for kind in range(2):
        for c in range(NC):
            def sent(k, carry, kind=kind, c=c):
                x_copy(kind, c, k).wait_send()
                return carry
            lax.fori_loop(0, feat - 1, sent, 0)


def body(feat, batch, features, tile_values, tile_blocks, tile_count, w_self, w_neigh, grad_out):
    rows, node_total = features.shape[1:]
    slots, width = tile_values.shape[1], tile_values.shape[-1]
    nodes, hid = grad_out.shape[1:]
    nb = node_total // width
    hi_n = 4
    mid_n = feat // (2 * hi_n)
    t = jnp.arange(slots, dtype=jnp.int32)
    key = jnp.where(t < tile_count[0], tile_blocks[0, 0], nb)
    full = key * slots + t
    rank = jnp.sum((full[None, :] < full[:, None]).astype(jnp.int32), axis=1)
    hit = rank[None, :] == t[:, None]
    tile_order = jnp.sum(jnp.where(hit, t[None, :], 0), axis=1)
    src_order = jnp.sum(jnp.where(hit, tile_blocks[0, 1][None, :], 0), axis=1)
    keys = jnp.sum(jnp.where(hit, key[None, :], 0), axis=1)
    d = jnp.arange(nb, dtype=jnp.int32)
    upto = jnp.sum((key[None, :] <= d[:, None]).astype(jnp.int32), axis=1)
    found = jnp.max((key[None, :] == d[:, None]).astype(jnp.int32), axis=1)
    last = jnp.where(found > 0, upto - 1, slots)

    dims = (feat, batch, hi_n, mid_n, rows, nodes, width, slots, hid)
    fr = feat * rows
    chunk = nodes // NC
    cb = 2 * hid // batch
    span = hi_n * rows
    s4_type = BF16 if batch == 2 else F32
    dma = pltpu.SemaphoreType.DMA
    any_spec = pl.BlockSpec(memory_space=pl.ANY)
    smem = pl.BlockSpec(memory_space=pltpu.SMEM)
    vmem = pl.BlockSpec(memory_space=pltpu.VMEM)
    hidden, grad_w = pl.pallas_call(
        functools.partial(kernel, dims),
        out_shape=(
            jax.ShapeDtypeStruct((nodes, hid), BF16),
            jax.ShapeDtypeStruct((rows, 2, hid), F32),
        ),
        in_specs=[smem] * 4 + [any_spec] * 5,
        out_specs=(vmem, vmem),
        scratch_shapes=[
            pltpu.VMEM((nb, rows, width), BF16),
            pltpu.VMEM((slots, width, width), BF16),
            pltpu.VMEM((2, fr, hid), BF16),
            pltpu.VMEM((nodes, hid), BF16),
            pltpu.VMEM((slots + 1, rows, width), BF16),
            pltpu.VMEM((NC, feat, rows, chunk), BF16),
            pltpu.VMEM((2, NC, fr, chunk), BF16),
            pltpu.VMEM((chunk, hid), F32),
            pltpu.VMEM((chunk, hid), BF16),
            pltpu.VMEM((fr, 2 * hid), F32),
            pltpu.VMEM((2, fr // 4, 2 * hid), F32),
            pltpu.VMEM((2, fr // 4, 2 * hid), F32),
            pltpu.VMEM((batch - 1, fr // 4, cb), BF16),
            pltpu.VMEM((batch - 1, fr // 4, cb), BF16),
            pltpu.VMEM((mid_n - 1, span // 2, 2 * hid), BF16),
            pltpu.VMEM((mid_n - 1, span // 2, 2 * hid), BF16),
            pltpu.VMEM((hi_n - 1, rows, cb), s4_type),
            pltpu.VMEM((hi_n - 1, rows, cb), s4_type),
            pltpu.VMEM((rows, cb), F32),
            pltpu.VMEM((batch - 1, rows, cb), F32),
            pltpu.VMEM((mid_n - 1, span // 2, cb), F32),
            pltpu.VMEM((mid_n - 1, span // 2, cb), F32),
            pltpu.VMEM((batch - 1, span // 2, cb), F32),
            pltpu.VMEM((batch - 1, span // 2, cb), F32),
            pltpu.VMEM((rows, 2 * hid), F32),
            dma((5,)),
            dma((NC,)),
            dma((2, NC, feat - 1)),
            dma((2, NC, feat)),
            dma((2, 2)),
            dma((2, batch - 1)),
            dma((2, mid_n - 1)),
            dma((2, hi_n - 1)),
            dma((2, batch - 1)),
            dma((2, mid_n - 1)),
            dma((2, batch - 1)),
        ],
        compiler_params=pltpu.CompilerParams(
            collective_id=0, has_side_effects=True, vmem_limit_bytes=58 * 1024 * 1024
        ),
    )(tile_order, src_order, keys, last, features[0], tile_values[0], w_self, w_neigh, grad_out[0])
    return hidden[None], grad_w


def solution(mesh):
    in_specs = (
        P("batch", "feat", None),
        P("batch", None, None, None),
        P("batch", None, None),
        P("batch"),
        P(),
        P(),
        P("batch", "feat", None),
    )
    out_specs = (P("batch", "feat", None), P("feat", None, None))
    fn = functools.partial(body, mesh.shape["feat"], mesh.shape["batch"])
    return jax.shard_map(fn, mesh=mesh, in_specs=in_specs, out_specs=out_specs, check_vma=False)
```

```python
import functools

import jax
import jax.numpy as jnp
from jax import lax
from jax.experimental import pallas as pl
from jax.experimental.pallas import tpu as pltpu
from jax.sharding import PartitionSpec as P

F32 = jnp.float32
BF16 = jnp.bfloat16
NC = 2
UNROLL = 8
NBLK = 256


def kernel(
    dims,
    tile_ref, src_ref, key_ref, last_ref, feat_hbm, tiles_hbm, ws_hbm, wn_hbm, go_hbm,
    hid_ref, gw_ref,
    feat_v, tiles_v, w_v, go_v, pref, msend, xs, pre_v, sg_v, grad,
    s1_send, s1_recv, s2_send, s2_recv, s3_send, s3_recv, s4_send, s4_recv, s5_send, s5_recv, s6_send, s6_recv, s7_send, s7_recv, gw_v,
    load_sem, own_sem, x_send, x_recv, s1_sems, s2_sems, s3_sems, s4_sems, s5_sems, s6_sems, s7_sems,
):
    feat, batch, hi_n, mid_n, rows, nodes, width, slots, hid = dims
    chunk = nodes // NC
    per_chunk = chunk // width
    blocks_per_dev = nodes // width
    me = lax.axis_index("feat")
    mb = lax.axis_index("batch")
    hi = me // (2 * mid_n)
    mid = (me // 2) % mid_n
    core = me % 2

    hf = hi_n // 2

    def slot_of(p):
        h = p // (2 * mid_n)
        return (p % 2) * (feat // 2) + (h // hf) * mid_n * hf + ((p // 2) % mid_n) * hf + h % hf

    my_rows = pl.ds(pl.multiple_of(slot_of(me) * rows, rows), rows)

    def peer(k):
        return (me + 1 + (k + feat // 2 - 1) % (feat - 1)) % feat

    loads = [
        pltpu.make_async_copy(tiles_hbm, tiles_v, load_sem.at[1]),
        pltpu.make_async_copy(go_hbm, go_v, load_sem.at[2]),
    ]
    for cp in loads:
        cp.start()

    barrier = pltpu.get_barrier_semaphore()

    def greet(k, carry):
        pl.semaphore_signal(barrier, inc=1, device_id={"feat": peer(k)}, device_id_type=pl.DeviceIdType.MESH)
        return carry

    lax.fori_loop(0, feat - 1, greet, 0)
    for j in range(1, batch):
        pl.semaphore_signal(
            barrier, inc=1, device_id={"batch": (mb + j) % batch}, device_id_type=pl.DeviceIdType.MESH
        )
    pl.semaphore_wait(barrier, feat - 1 + batch - 1)

    def x_copy(kind, c, k):
        p = peer(k)
        if kind == 0:
            start = pl.multiple_of(p * nodes + c * chunk, chunk)
            src = feat_hbm.at[:, pl.ds(start, chunk)]
        else:
            src = msend.at[c, p]
        return pltpu.make_async_remote_copy(
            src_ref=src,
            dst_ref=xs.at[kind, c, my_rows, :],
            send_sem=x_send.at[kind, c, k],
            recv_sem=x_recv.at[kind, c, me],
            device_id={"feat": p},
            device_id_type=pl.DeviceIdType.MESH,
        )

    for c in range(NC):
        def send_feat(k, carry, c=c):
            x_copy(0, c, k).start()
            return carry
        lax.fori_loop(0, feat - 1, send_feat, 0)

    def load_block(i, carry):
        at = pl.ds(pl.multiple_of(i * width, width), width)
        pltpu.make_async_copy(feat_hbm.at[:, at], feat_v.at[i], load_sem.at[0]).start()
        return carry

    lax.fori_loop(0, feat * blocks_per_dev, load_block, 0)
    owns = []
    for c in range(NC):
        start = pl.multiple_of(me * nodes + c * chunk, chunk)
        cp = pltpu.make_async_copy(feat_hbm.at[:, pl.ds(start, chunk)], xs.at[0, c, my_rows, :], own_sem.at[c])
        cp.start()
        owns.append(cp)
    for w, hbm in enumerate((ws_hbm, wn_hbm)):
        for p in range(feat):
            s = slot_of(p)
            pltpu.make_async_copy(
                hbm.at[pl.ds(p * rows, rows), :], w_v.at[w, pl.ds(s * rows, rows), :], load_sem.at[3 + w]
            ).start()

    pltpu.make_async_copy(feat_v, feat_v, load_sem.at[0]).wait()
    loads[0].wait()

    ones = jnp.ones((16, width), BF16)

    pref[slots] = jnp.zeros((rows, width), BF16)

    def group(g, acc):
        for u in range(UNROLL):
            t = g * UNROLL + u
            lhs = jnp.concatenate([feat_v[src_ref[t]], ones], axis=0)
            res = lax.dot_general(lhs, tiles_v[tile_ref[t]], (((1,), (1,)), ((), ())), preferred_element_type=F32)
            same = 1 - jnp.minimum(key_ref[t] - key_ref[jnp.maximum(t - 1, 0)], 1)
            acc = acc * same.astype(F32) + res
            inv = 1.0 / jnp.maximum(acc[rows:rows + 8], 1.0)
            mean = acc[:rows].reshape(rows // 8, 8, width) * inv[None]
            pref[t] = mean.reshape(rows, width).astype(BF16)
        return acc

    lax.fori_loop(0, slots // UNROLL, group, jnp.zeros((rows + 16, width), F32))

    def mean_block(c, p, b):
        d = p * blocks_per_dev + c * per_chunk + b
        return pref[last_ref[d]]

    for c in range(NC):
        def send_mean(k, carry, c=c):
            p = peer(k)
            for b in range(per_chunk):
                msend[c, p, :, b * width:(b + 1) * width] = mean_block(c, p, b)
            x_copy(1, c, k).start()
            return carry
        lax.fori_loop(0, feat - 1, send_mean, 0)
        for b in range(per_chunk):
            xs[1, c, my_rows, b * width:(b + 1) * width] = mean_block(c, me, b)

    for cp in owns:
        cp.wait()
    loads[1].wait()
    for w, hbm in enumerate((ws_hbm, wn_hbm)):
        pltpu.make_async_copy(hbm, w_v.at[w], load_sem.at[3 + w]).wait()

    def wait_x(kind, c):
        def one(k, carry):
            p = peer(k)
            pltpu.make_async_remote_copy(
                src_ref=msend.at[c, p],
                dst_ref=xs.at[kind, c, pl.ds(pl.multiple_of(slot_of(p) * rows, rows), rows), :],
                send_sem=x_send.at[kind, c, k],
                recv_sem=x_recv.at[kind, c, p],
                device_id={"feat": p},
                device_id_type=pl.DeviceIdType.MESH,
            ).wait_recv()
            return carry
        lax.fori_loop(0, feat - 1, one, 0)

    tn = (((0,), (0,)), ((), ()))
    fr = feat * rows
    half = fr // 2

    for c in range(NC):
        wait_x(0, c)

        def self_part(i, carry, c=c):
            at = pl.ds(pl.multiple_of(i * NBLK, NBLK), NBLK)
            pre_v[at, :] = lax.dot_general(xs[0, c, :, at], w_v[0], tn, preferred_element_type=F32)
            return carry

        lax.fori_loop(0, chunk // NBLK, self_part, 0)
        wait_x(1, c)

        def neigh_part(i, carry, c=c):
            at = pl.ds(pl.multiple_of(i * NBLK, NBLK), NBLK)
            pre = pre_v[at, :] + lax.dot_general(xs[1, c, :, at], w_v[1], tn, preferred_element_type=F32)
            e = jnp.exp(jnp.minimum(pre, 0.0))
            row = pl.ds(pl.multiple_of(c * chunk + i * NBLK, NBLK), NBLK)
            hid_ref[row, :] = (jnp.maximum(pre, 0.0) + (e - 1.0)).astype(BF16)
            sg_v[at, :] = (go_v[row, :].astype(F32) * e).astype(BF16)
            return carry

        lax.fori_loop(0, chunk // NBLK, neigh_part, 0)

        if c < NC - 1:
            for kind in range(2):
                def grads(i, carry, c=c, kind=kind):
                    at = pl.ds(pl.multiple_of(i * NBLK, NBLK), NBLK)
                    cols = pl.ds(kind * hid, hid)
                    g = jnp.dot(xs[kind, c, at, :], sg_v[...], preferred_element_type=F32)
                    if c > 0:
                        g = g + grad[at, cols]
                    grad[at, cols] = g
                    return carry
                lax.fori_loop(0, fr // NBLK, grads, 0)

    c = NC - 1

    def last_grads(base, i):
        at = pl.ds(pl.multiple_of(base + (i // 2) * NBLK, NBLK), NBLK)
        cols = pl.ds(pl.multiple_of((i % 2) * hid, hid), hid)
        return at, cols, grad[at, cols] + jnp.dot(xs[i % 2, c, at, :], sg_v[...], preferred_element_type=F32)

    quarter = half // 2
    steps = 2 * quarter // NBLK
    first = []
    for f in range(2):
        def away(i, carry, f=f):
            _, cols, g = last_grads((1 - core) * half + f * quarter, i)
            s1_send[f, pl.ds(pl.multiple_of((i // 2) * NBLK, NBLK), NBLK), cols] = g
            return carry
        lax.fori_loop(0, steps, away, 0)
        cp = pltpu.make_async_remote_copy(
            src_ref=s1_send.at[f], dst_ref=s1_recv.at[f],
            send_sem=s1_sems.at[0, f], recv_sem=s1_sems.at[1, f],
            device_id={"feat": me + 1 - 2 * core}, device_id_type=pl.DeviceIdType.MESH,
        )
        cp.start()
        first.append(cp)

    def home(i, carry):
        at, cols, g = last_grads(core * half, i)
        grad[at, cols] = g
        return carry

    lax.fori_loop(0, 2 * steps, home, 0)

    def add_core(f):
        first[f].wait_recv()

        def add1(i, carry):
            at = pl.ds(pl.multiple_of(core * half + f * quarter + i * 64, 64), 64)
            grad[at, :] = grad[at, :] + s1_recv[f, pl.ds(pl.multiple_of(i * 64, 64), 64), :]
            return carry

        lax.fori_loop(0, quarter // 64, add1, 0)

    pending = []

    cb = 2 * hid // batch
    part = hf * rows

    def cols_of(b):
        return pl.ds(pl.multiple_of(b * cb, cb), cb)

    def flow_rows(f):
        return pl.ds(pl.multiple_of(core * half + f * quarter, quarter), quarter)

    def mid_rows(f, m):
        return pl.ds(pl.multiple_of(core * half + f * quarter + m * part, part), part)

    def hi_rows(h):
        return pl.ds(
            pl.multiple_of(core * half + (h // hf) * quarter + mid * part + (h % hf) * rows, rows), rows
        )

    every = pl.ds(0, 2 * hid)

    def to_batch(b):
        return {"batch": b}

    def to_mid(m):
        return {"feat": hi * 2 * mid_n + m * 2 + core}

    def to_hi(h):
        return {"feat": h * 2 * mid_n + mid * 2 + core}

    def send_parts(size, mine, place, where, send, recv, sems):
        copies = []
        for j in range(1, size):
            to = (mine + j) % size
            at, cols = where(to)
            send[j - 1] = grad[at, cols].astype(send.dtype)
            cp = pltpu.make_async_remote_copy(
                src_ref=send.at[j - 1], dst_ref=recv.at[j - 1],
                send_sem=sems.at[0, j - 1], recv_sem=sems.at[1, j - 1],
                device_id=place(to), device_id_type=pl.DeviceIdType.MESH,
            )
            cp.start()
            copies.append(cp)
        pending.extend(copies)
        return copies

    def add_parts(copies, where, recv):
        at, cols = where
        total = grad[at, cols]
        for j, cp in enumerate(copies):
            cp.wait_recv()
            total = total + recv[j].astype(F32)
        grad[at, cols] = total
        return total

    wb0 = lambda b: (flow_rows(0), cols_of(b))
    wm1 = lambda m: (mid_rows(1, m), every)
    wm0 = lambda m: (mid_rows(0, m), cols_of(mb))
    wb1 = lambda b: (mid_rows(1, mid), cols_of(b))
    add_core(0)
    first_b = send_parts(batch, mb, to_batch, wb0, s2_send, s2_recv, s2_sems)
    add_core(1)
    first_m = send_parts(mid_n, mid, to_mid, wm1, s3_send, s3_recv, s3_sems)
    add_parts(first_b, wb0(mb), s2_recv)
    second_m = send_parts(mid_n, mid, to_mid, wm0, s6_send, s6_recv, s6_sems)
    add_parts(first_m, wm1(mid), s3_recv)
    second_b = send_parts(batch, mb, to_batch, wb1, s7_send, s7_recv, s7_sems)
    add_parts(second_m, wm0(mid), s6_recv)
    add_parts(second_b, wb1(mb), s7_recv)
    wh = lambda h: (hi_rows(h), cols_of(mb))
    across = send_parts(hi_n, hi, to_hi, wh, s4_send, s4_recv, s4_sems)
    total4 = add_parts(across, wh(hi), s4_recv)
    s5_send[...] = total4
    gather = []
    for j in range(1, batch):
        cp = pltpu.make_async_remote_copy(
            src_ref=s5_send, dst_ref=s5_recv.at[j - 1],
            send_sem=s5_sems.at[0, j - 1], recv_sem=s5_sems.at[1, j - 1],
            device_id={"batch": (mb + j) % batch}, device_id_type=pl.DeviceIdType.MESH,
        )
        cp.start()
        gather.append(cp)
    gw_v[:, cols_of(mb)] = total4
    for j in range(1, batch):
        gather[j - 1].wait_recv()
        gw_v[:, cols_of((mb + batch - j) % batch)] = s5_recv[j - 1]
    for kind in range(2):
        gw_ref[:, kind, :] = gw_v[:, kind * hid:(kind + 1) * hid]

    for cp in first + pending + gather:
        cp.wait_send()
    for kind in range(2):
        for c in range(NC):
            def sent(k, carry, kind=kind, c=c):
                x_copy(kind, c, k).wait_send()
                return carry
            lax.fori_loop(0, feat - 1, sent, 0)


def body(feat, batch, features, tile_values, tile_blocks, tile_count, w_self, w_neigh, grad_out):
    rows, node_total = features.shape[1:]
    slots, width = tile_values.shape[1], tile_values.shape[-1]
    nodes, hid = grad_out.shape[1:]
    nb = node_total // width
    hi_n = 4
    mid_n = feat // (2 * hi_n)
    t = jnp.arange(slots, dtype=jnp.int32)
    key = jnp.where(t < tile_count[0], tile_blocks[0, 0], nb)
    full = key * slots + t
    rank = jnp.sum((full[None, :] < full[:, None]).astype(jnp.int32), axis=1)
    hit = rank[None, :] == t[:, None]
    packed = (t << 18) | (tile_blocks[0, 1] << 9) | key
    packed = jnp.sum(jnp.where(hit, packed[None, :], 0), axis=1)
    tile_order, src_order, keys = packed >> 18, (packed >> 9) & 511, packed & 511
    d = jnp.arange(nb, dtype=jnp.int32)
    upto = jnp.sum((key[None, :] <= d[:, None]).astype(jnp.int32), axis=1)
    found = jnp.max((key[None, :] == d[:, None]).astype(jnp.int32), axis=1)
    last = jnp.where(found > 0, upto - 1, slots)

    dims = (feat, batch, hi_n, mid_n, rows, nodes, width, slots, hid)
    fr = feat * rows
    chunk = nodes // NC
    cb = 2 * hid // batch
    span = hi_n * rows
    s4_type = BF16 if batch == 2 else F32
    dma = pltpu.SemaphoreType.DMA
    any_spec = pl.BlockSpec(memory_space=pl.ANY)
    smem = pl.BlockSpec(memory_space=pltpu.SMEM)
    vmem = pl.BlockSpec(memory_space=pltpu.VMEM)
    hidden, grad_w = pl.pallas_call(
        functools.partial(kernel, dims),
        out_shape=(
            jax.ShapeDtypeStruct((nodes, hid), BF16),
            jax.ShapeDtypeStruct((rows, 2, hid), F32),
        ),
        in_specs=[smem] * 4 + [any_spec] * 5,
        out_specs=(vmem, vmem),
        scratch_shapes=[
            pltpu.VMEM((nb, rows, width), BF16),
            pltpu.VMEM((slots, width, width), BF16),
            pltpu.VMEM((2, fr, hid), BF16),
            pltpu.VMEM((nodes, hid), BF16),
            pltpu.VMEM((slots + 1, rows, width), BF16),
            pltpu.VMEM((NC, feat, rows, chunk), BF16),
            pltpu.VMEM((2, NC, fr, chunk), BF16),
            pltpu.VMEM((chunk, hid), F32),
            pltpu.VMEM((chunk, hid), BF16),
            pltpu.VMEM((fr, 2 * hid), F32),
            pltpu.VMEM((2, fr // 4, 2 * hid), F32),
            pltpu.VMEM((2, fr // 4, 2 * hid), F32),
            pltpu.VMEM((batch - 1, fr // 4, cb), BF16),
            pltpu.VMEM((batch - 1, fr // 4, cb), BF16),
            pltpu.VMEM((mid_n - 1, span // 2, 2 * hid), BF16),
            pltpu.VMEM((mid_n - 1, span // 2, 2 * hid), BF16),
            pltpu.VMEM((hi_n - 1, rows, cb), s4_type),
            pltpu.VMEM((hi_n - 1, rows, cb), s4_type),
            pltpu.VMEM((rows, cb), F32),
            pltpu.VMEM((batch - 1, rows, cb), F32),
            pltpu.VMEM((mid_n - 1, span // 2, cb), F32),
            pltpu.VMEM((mid_n - 1, span // 2, cb), F32),
            pltpu.VMEM((batch - 1, span // 2, cb), F32),
            pltpu.VMEM((batch - 1, span // 2, cb), F32),
            pltpu.VMEM((rows, 2 * hid), F32),
            dma((5,)),
            dma((NC,)),
            dma((2, NC, feat - 1)),
            dma((2, NC, feat)),
            dma((2, 2)),
            dma((2, batch - 1)),
            dma((2, mid_n - 1)),
            dma((2, hi_n - 1)),
            dma((2, batch - 1)),
            dma((2, mid_n - 1)),
            dma((2, batch - 1)),
        ],
        compiler_params=pltpu.CompilerParams(
            collective_id=0, has_side_effects=True, vmem_limit_bytes=58 * 1024 * 1024
        ),
    )(tile_order, src_order, keys, last, features[0], tile_values[0], w_self, w_neigh, grad_out[0])
    return hidden[None], grad_w


def solution(mesh):
    in_specs = (
        P("batch", "feat", None),
        P("batch", None, None, None),
        P("batch", None, None),
        P("batch"),
        P(),
        P(),
        P("batch", "feat", None),
    )
    out_specs = (P("batch", "feat", None), P("feat", None, None))
    fn = functools.partial(body, mesh.shape["feat"], mesh.shape["batch"])
    return jax.shard_map(fn, mesh=mesh, in_specs=in_specs, out_specs=out_specs, check_vma=False)
```
